32 devices in a mesh: dp: 8 (over z, y), co: 4 (over x, core).
Axes of the slice: x: 2, y: 2, z: 4, core: 2. Of those that a mesh axis runs over, the one named last changes fastest.
Arguments:
- embeddings: bfloat16 [3072, 1024], P(('dp', 'co')), may hold values from -2500 to 2500
- labels: int32 [3072], P(('dp', 'co')), may hold values from 0 to 63, as said below
- ranks: int32 [3072], P(('dp', 'co')), may hold values from 0 to 3071, each once
Outputs:
- max_cosine: float32 [3072], P(('dp', 'co'))
The draws below stay inside these ranges and needn't reach their ends.
Inputs may be any that keep to these rules, and one draw needn't show every extreme that they name: The rows of one device hold at most 24 rows whose labels // 8 name one owner; in every draw some owner gets exactly 24 rows from every device.
All inputs are finite; a program needn't handle non-finite values.
Results may differ from the reference program's by a relative error of at most 0.00061.
Values may be sent and summed in bfloat16 or wider, within the bound.
A program may use at most 64 MiB of HBM per device.

```python
import math
import jax
import jax.numpy as jnp
from jax import lax

D = 1024
ROWS_DEV = 96
CL_DEV = 8
CAP = 24
ROWS = 3072
CLUSTERS = 64
N_DP = 8


def route_labels(key):
    hot_owner = jax.random.randint(jax.random.fold_in(key, 5), (), 0, N_DP).astype(jnp.int32)
    base_key = jax.random.fold_in(key, 6)

    def one_device(index):
        device_key = jax.random.fold_in(base_key, index)
        first_key, second_key, third_key, fourth_key = jax.random.split(device_key, 4)
        owner_order = jax.random.permutation(first_key, N_DP).astype(jnp.int32)
        owner_order = jnp.where(owner_order == hot_owner, owner_order[0], owner_order).at[0].set(hot_owner)
        spare = jax.random.permutation(second_key, (N_DP - 1) * CAP)[:ROWS_DEV - CAP].astype(jnp.int32)
        owners = jnp.concatenate([jnp.full((CAP,), 1, jnp.int32) * hot_owner, owner_order[1 + spare // CAP]])
        owners = owners[jax.random.permutation(third_key, ROWS_DEV)]
        local = jax.random.randint(fourth_key, (ROWS_DEV,), 0, CL_DEV).astype(jnp.int32)
        return (owners * CL_DEV + local).astype(jnp.int32)
    return jax.vmap(one_device)(jnp.arange(ROWS // ROWS_DEV, dtype=jnp.int32)).reshape(-1)


def draw_labels(key, part):
    return route_labels(key)


def draw_embeddings(key, part):
    labels = route_labels(key)
    key = jax.random.fold_in(key, 11)
    keys = jax.random.split(key, 5)
    centers = jnp.clip(jax.random.normal(keys[0], (CLUSTERS, D), jnp.float32), -4.0, 4.0)
    strength = jnp.exp(jax.random.uniform(keys[1], (CLUSTERS,), jnp.float32, math.log(0.4), math.log(2.5)))
    noise = jnp.clip(jax.random.normal(keys[2], (ROWS, D), jnp.float32), -4.0, 4.0)
    row_scale = jnp.exp(jax.random.uniform(keys[3], (ROWS, 1), jnp.float32, 0.0, math.log(10.0)))
    column_scale = jnp.exp(jax.random.uniform(keys[4], (1, D), jnp.float32, 0.0, math.log(10.0)))
    values = row_scale * column_scale * (strength[labels][:, None] * centers[labels] + noise)
    return values.astype(jnp.bfloat16)


def setup_inputs(seed: int = 0) -> dict:
    arg_keys = jax.random.split(jax.random.key(seed), 4)
    return {
        "embeddings": draw_embeddings(jax.random.fold_in(arg_keys[3], 71), 0),
        "labels": draw_labels(jax.random.fold_in(arg_keys[3], 71), 0),
        "ranks": jax.random.permutation(arg_keys[2], ROWS).astype(jnp.int32),
    }


EPSILON = 1e-06

def reference(embeddings, labels, ranks):
    values = embeddings.astype(jnp.float32)
    unit = (values * lax.rsqrt(lax.optimization_barrier(jnp.sum(values * values, axis=1, keepdims=True)) + EPSILON)).astype(jnp.bfloat16)
    total = labels.shape[0]
    block = min(512, total)
    count = (total + block - 1) // block
    padded = count * block
    sort_key = labels.astype(jnp.int32) * total + ranks.astype(jnp.int32)
    order = jnp.argsort(sort_key).astype(jnp.int32)
    sorted_unit = jnp.concatenate([unit[order], jnp.zeros((padded - total, D), unit.dtype)], axis=0)
    sorted_label = jnp.concatenate([labels[order], jnp.full((padded - total,), CLUSTERS, jnp.int32)])
    sorted_rank = jnp.concatenate([ranks[order], jnp.zeros((padded - total,), jnp.int32)])
    first_member = jnp.searchsorted(sorted_label, sorted_label, side='left').astype(jnp.int32)

    def one_block(index):
        begin = index * block
        query = lax.dynamic_slice_in_dim(sorted_unit, begin, block, 0)
        query_label = lax.dynamic_slice_in_dim(sorted_label, begin, block, 0)
        query_rank = lax.dynamic_slice_in_dim(sorted_rank, begin, block, 0)
        reach = (begin - first_member[begin] + block - 1) // block

        def absorb(step, best):
            key_begin = (index - step) * block
            keys = lax.dynamic_slice_in_dim(sorted_unit, key_begin, block, 0)
            key_label = lax.dynamic_slice_in_dim(sorted_label, key_begin, block, 0)
            key_rank = lax.dynamic_slice_in_dim(sorted_rank, key_begin, block, 0)
            scores = jnp.dot(query, keys.T, preferred_element_type=jnp.float32)
            linked = (query_label[:, None] == key_label[None, :]) & (key_rank[None, :] < query_rank[:, None])
            return jnp.maximum(best, lax.optimization_barrier(jnp.max(jnp.where(linked, scores, -1.0), axis=1)))
        return lax.fori_loop(0, reach + 1, absorb, jnp.full((block,), -1.0, jnp.float32))
    best = lax.map(one_block, jnp.arange(count, dtype=jnp.int32)).reshape(-1)[:total]
    return jnp.zeros((total,), jnp.float32).at[order].set(best)
```

```python
import functools

import jax
import jax.numpy as jnp
from jax import lax
from jax.experimental import pallas as pl
from jax.experimental.pallas import tpu as pltpu
from jax.sharding import PartitionSpec as P

CL_DEV = 8


EPSILON = 1e-06


def match_best(best, mine_rows, mine_label, mine_rank, other_rows, other_label, other_rank):
    scores = lax.dot_general(
        mine_rows, other_rows, (((1,), (1,)), ((), ())), preferred_element_type=jnp.float32
    )
    linked = (
        (mine_label[:, None] == other_label[None, :])
        & (other_label[None, :] >= 0)
        & (other_rank[None, :] < mine_rank[:, None])
    )
    return jnp.maximum(best, jnp.max(jnp.where(linked, scores, -1.0), axis=1))


def local(embeddings, labels, ranks):
    row_count, width = embeddings.shape
    owner_count = lax.axis_size("dp")
    slot_cap = max(2, 2 * row_count // owner_count)
    slot_total = owner_count * slot_cap
    values = embeddings.astype(jnp.float32)
    unit = (values * lax.rsqrt(jnp.sum(values * values, axis=1, keepdims=True) + EPSILON)).astype(
        jnp.bfloat16
    )
    owner = labels // CL_DEV
    onehot = (owner[:, None] == jnp.arange(owner_count, dtype=jnp.int32)[None, :]).astype(
        jnp.float32
    )
    lower = (jnp.arange(row_count)[:, None] >= jnp.arange(row_count)[None, :]).astype(jnp.float32)
    running = jnp.dot(lower, onehot, preferred_element_type=jnp.float32)
    position = (jnp.sum(running * onehot, axis=1) - 1.0).astype(jnp.int32)
    slot = owner * slot_cap + position
    send_rows = (
        jnp.zeros((slot_total, width), jnp.bfloat16)
        .at[slot]
        .set(unit)
        .reshape(owner_count, slot_cap, width)
    )
    send_label = (
        jnp.full((slot_total,), -1, jnp.int32).at[slot].set(labels).reshape(owner_count, slot_cap)
    )
    send_rank = (
        jnp.zeros((slot_total,), jnp.int32).at[slot].set(ranks).reshape(owner_count, slot_cap)
    )
    start_best = jnp.full((slot_total,), -1.0, jnp.float32)
    group_rows, group_label, group_rank = (
        lax.all_gather(send_rows, "co", axis=1, tiled=True),
        lax.all_gather(send_label, "co", axis=1, tiled=True),
        lax.all_gather(send_rank, "co", axis=1, tiled=True),
    )
    got_rows, got_label, got_rank = (
        lax.all_to_all(group_rows, "dp", split_axis=0, concat_axis=0, tiled=True),
        lax.all_to_all(group_label, "dp", split_axis=0, concat_axis=0, tiled=True),
        lax.all_to_all(group_rank, "dp", split_axis=0, concat_axis=0, tiled=True),
    )
    offset = lax.axis_index("co") * slot_cap
    mine_rows = lax.dynamic_slice_in_dim(got_rows, offset, slot_cap, 1).reshape(slot_total, width)
    mine_label = lax.dynamic_slice_in_dim(got_label, offset, slot_cap, 1).reshape(slot_total)
    mine_rank = lax.dynamic_slice_in_dim(got_rank, offset, slot_cap, 1).reshape(slot_total)
    best = match_best(
        start_best,
        mine_rows,
        mine_label,
        mine_rank,
        got_rows.reshape(-1, width),
        got_label.reshape(-1),
        got_rank.reshape(-1),
    )
    returned = lax.all_to_all(
        best.reshape(owner_count, slot_cap), "dp", split_axis=0, concat_axis=0, tiled=True
    )
    return returned.reshape(slot_total)[slot]


MESH = pl.DeviceIdType.MESH
HIGHEST = lax.Precision.HIGHEST


def iota(shape, dim):
    return lax.broadcasted_iota(jnp.int32, shape, dim)


def owner_place(owner, n_dp, n_co):
    half = n_dp // 2
    return n_dp // 4 + lax.rem(owner, half), (owner // half) * (n_co // 2)


def kernel(
    n_dp, n_co, cap, shift,
    emb_ref, label_ref, rank_ref, out_ref,
    send, recv, key_send, key_recv, rows, ret_send, ret_recv,
    send_sem, recv_sem, key_send_sem, key_recv_sem, ret_send_sem, ret_recv_sem,
):
    n_dev = n_dp * n_co
    n_owner = n_dp
    row_count, width = emb_ref.shape
    half = width // 2
    total = n_dev * cap
    my_dp, my_co = lax.axis_index("dp"), lax.axis_index("co")
    me = my_dp * n_co + my_co
    mid = n_dp // 4
    is_owner = (my_dp >= mid) & (my_dp < mid + n_dp // 2) & (lax.rem(my_co, n_co // 2) == 0)
    my_owner = (my_co // (n_co // 2)) * (n_dp // 2) + my_dp - mid

    barrier = pltpu.get_barrier_semaphore()

    def greet(j, _):
        @pl.when(j != me)
        def _():
            pl.semaphore_signal(
                barrier, inc=1, device_id=(j // n_co, lax.rem(j, n_co)), device_id_type=MESH
            )
        return 0

    @pl.when(is_owner)
    def _():
        lax.fori_loop(0, n_dev, greet, 0)

    @pl.when(jnp.logical_not(is_owner))
    def _():
        def greet_owner(o, _):
            pl.semaphore_signal(
                barrier, inc=1, device_id=owner_place(o, n_dp, n_co), device_id_type=MESH
            )
            return 0

        lax.fori_loop(0, n_owner, greet_owner, 0)

    values = emb_ref[...].astype(jnp.float32)
    unit = (values * lax.rsqrt(jnp.sum(values * values, axis=1, keepdims=True) + EPSILON)).astype(
        jnp.bfloat16
    )
    square = (row_count, row_count)
    down, across = iota(square, 0), iota(square, 1)
    label_row = label_ref[...]
    key_row = label_row * (1 << shift) + rank_ref[...]
    owner_row = label_row // CL_DEV
    diagonal = down == across

    def to_column(row):
        return jnp.sum(jnp.where(diagonal, row, 0), axis=1, keepdims=True)

    owner_col, key_col = to_column(owner_row), to_column(key_row)
    same = owner_col == owner_row
    place_row = jnp.sum(jnp.where(same & (down < across), 1, 0), axis=0, keepdims=True)
    place_col = jnp.sum(jnp.where(same & (across < down), 1, 0), axis=1, keepdims=True)

    @pl.when(is_owner)
    def _():
        pl.semaphore_wait(barrier, n_dev - 1)

    @pl.when(jnp.logical_not(is_owner))
    def _():
        pl.semaphore_wait(barrier, n_owner)

    def to_owner(step):
        owner = lax.rem(me + step, n_owner)
        dp, co = owner_place(owner, n_dp, n_co)
        here = (dp == my_dp) & (co == my_co)
        copies = [
            pltpu.make_async_remote_copy(
                src_ref=a.at[step], dst_ref=b.at[me], send_sem=x.at[step], recv_sem=y.at[me],
                device_id=(dp, co), device_id_type=MESH,
            )
            for a, b, x, y in (
                (key_send, key_recv, key_send_sem, key_recv_sem),
                (send, recv, send_sem, recv_sem),
            )
        ]
        local_copies = [
            pltpu.make_async_copy(a.at[step], b.at[me], y.at[me])
            for a, b, y in ((key_send, key_recv, key_recv_sem), (send, recv, recv_sem))
        ]
        return owner, here, copies, local_copies

    lane = iota((row_count, 128), 1)
    my_sublane = iota((8, 128), 0) == lax.rem(me, 8)
    slot = iota((2 * cap, row_count), 0)
    for step in range(n_owner):
        owner, here, copies, local_copies = to_owner(step)
        keys = jnp.sum(
            jnp.where((owner_col == owner) & (place_col == lane), key_col + 1, 0),
            axis=0, keepdims=True,
        ) - 1
        key_send[step] = jnp.where(my_sublane, keys, 0).astype(jnp.float32)
        position = jnp.where(owner_row == owner, place_row, -2 * cap)
        low = jnp.where(slot == position, 1.0, 0.0).astype(jnp.bfloat16)
        high = jnp.where(slot == position + cap, 1.0, 0.0).astype(jnp.bfloat16)
        picked = jnp.dot(low, unit[:, :half], preferred_element_type=jnp.float32) + jnp.dot(
            high, unit[:, half:], preferred_element_type=jnp.float32
        )
        send[step] = picked.astype(jnp.bfloat16)

        @pl.when(here)
        def _():
            for copy in local_copies:
                copy.start()

        @pl.when(jnp.logical_not(here))
        def _():
            for copy in copies:
                copy.start()

    @pl.when(is_owner)
    def _():
        every = iota((128, total), 1)
        source = jnp.floor((every.astype(jnp.float32) + 0.5) * (1.0 / cap)).astype(jnp.int32)
        spread = jnp.where(every - source * cap == iota((128, total), 0), 1.0, 0.0)
        every_t = iota((total, 128), 0)
        source_t = jnp.floor((every_t.astype(jnp.float32) + 0.5) * (1.0 / cap)).astype(jnp.int32)
        spread_t = jnp.where(every_t - source_t * cap == iota((total, 128), 1), 1.0, 0.0)
        from_row = source[:n_dev] == iota((n_dev, total), 0)
        from_col = source_t[:, :n_dev] == iota((total, n_dev), 1)

        def wait(kind, sem):
            def one(j, _):
                pltpu.make_async_copy(kind.at[j], kind.at[j], sem.at[j]).wait()
                return 0

            return one

        lax.fori_loop(0, n_dev, wait(key_recv, key_recv_sem), 0)
        table = jnp.sum(key_recv[...].reshape(n_dev // 8, 8, 8, 128), axis=1).reshape(n_dev, 128)
        keys_row = jnp.sum(
            jnp.where(
                from_row,
                jnp.dot(table, spread, precision=HIGHEST, preferred_element_type=jnp.float32),
                0.0,
            ),
            axis=0, keepdims=True,
        )
        keys_col = jnp.sum(
            jnp.where(
                from_col,
                lax.dot_general(
                    spread_t, table, (((1,), (1,)), ((), ())),
                    precision=HIGHEST, preferred_element_type=jnp.float32,
                ),
                0.0,
            ),
            axis=1, keepdims=True,
        )
        keys_row = jnp.round(keys_row)
        keys_col = jnp.round(keys_col)
        first_row = jnp.floor(keys_row * (1.0 / (1 << shift))) * (1 << shift)
        first_row = jnp.maximum(first_row, 0.0)

        for pair in range(n_dev // 2):
            two = []
            for j in (2 * pair, 2 * pair + 1):
                pltpu.make_async_copy(recv.at[j], recv.at[j], recv_sem.at[j]).wait()
                two.append(recv[j].astype(jnp.float32))
            block = pl.ds(pair * 2 * cap, 2 * cap)
            rows[block, :half] = jnp.concatenate([x[:cap] for x in two], axis=0).astype(jnp.bfloat16)
            rows[block, half:] = jnp.concatenate([x[cap:] for x in two], axis=0).astype(jnp.bfloat16)

        best = jnp.full((1, total), -1.0, jnp.float32)
        tall = total // 3 if total % 48 == 0 else total
        for begin in range(0, total, tall):
            scores = lax.dot_general(
                rows[begin : begin + tall, :], rows[...], (((1,), (1,)), ((), ())),
                preferred_element_type=jnp.float32,
            )
            other = keys_col[begin : begin + tall]
            linked = (other < keys_row) & (other >= first_row)
            best = jnp.maximum(
                best, jnp.max(jnp.where(linked, scores, -1.0), axis=0, keepdims=True)
            )
        ret_send[...] = lax.dot_general(
            jnp.where(from_row, best, 0.0), spread, (((1,), (1,)), ((), ())),
            precision=HIGHEST, preferred_element_type=jnp.float32,
        ).reshape(n_dev // 8, 8, 128)

        def back(j):
            return pltpu.make_async_remote_copy(
                src_ref=ret_send.at[j // 8], dst_ref=ret_recv.at[my_owner],
                send_sem=ret_send_sem.at[j], recv_sem=ret_recv_sem.at[my_owner],
                device_id=(j // n_co, lax.rem(j, n_co)), device_id_type=MESH,
            )

        def home(j):
            return pltpu.make_async_copy(
                ret_send.at[j // 8], ret_recv.at[my_owner], ret_recv_sem.at[my_owner]
            )

        def give(j, _):
            @pl.when(j != me)
            def _():
                back(j).start()

            @pl.when(j == me)
            def _():
                home(j).start()
            return 0

        lax.fori_loop(0, n_dev, give, 0)

        def given(j, _):
            @pl.when(j != me)
            def _():
                back(j).wait_send()
            return 0

        lax.fori_loop(0, n_dev, given, 0)

    for step in range(n_owner):
        _, here, copies, _ = to_owner(step)

        @pl.when(jnp.logical_not(here))
        def _():
            for copy in copies:
                copy.wait_send()

    for o in range(n_owner):
        pltpu.make_async_copy(ret_recv.at[o], ret_recv.at[o], ret_recv_sem.at[o]).wait()
    mine = jnp.sum(jnp.where(my_sublane[None], ret_recv[...], 0.0), axis=1)
    chosen = jnp.where(owner_row == iota((n_owner, row_count), 0), 1.0, 0.0)
    by_place = lax.dot_general(
        mine, chosen, (((0,), (0,)), ((), ())),
        precision=HIGHEST, preferred_element_type=jnp.float32,
    )
    out_ref[...] = jnp.sum(
        jnp.where(iota((128, row_count), 0) == place_row, by_place, 0.0), axis=0, keepdims=True
    )


def local_fused(n_dp, n_co, embeddings, labels, ranks):
    row_count, width = embeddings.shape
    cap = max(2, 2 * row_count // n_dp)
    n_dev = n_dp * n_co
    shift = (row_count * n_dev - 1).bit_length()
    dma = pltpu.SemaphoreType.DMA
    out = pl.pallas_call(
        functools.partial(kernel, n_dp, n_co, cap, shift),
        out_shape=jax.ShapeDtypeStruct((1, row_count), jnp.float32),
        in_specs=[pl.BlockSpec(memory_space=pltpu.VMEM)] * 3,
        out_specs=pl.BlockSpec(memory_space=pltpu.VMEM),
        scratch_shapes=[
            pltpu.VMEM((n_dp, 2 * cap, width // 2), jnp.bfloat16),
            pltpu.VMEM((n_dev, 2 * cap, width // 2), jnp.bfloat16),
            pltpu.VMEM((n_dp, 8, 128), jnp.float32),
            pltpu.VMEM((n_dev, 8, 128), jnp.float32),
            pltpu.VMEM((n_dev * cap, width), jnp.bfloat16),
            pltpu.VMEM((n_dev // 8, 8, 128), jnp.float32),
            pltpu.VMEM((n_dp, 8, 128), jnp.float32),
            dma((n_dp,)), dma((n_dev,)), dma((n_dp,)), dma((n_dev,)), dma((n_dev,)), dma((n_dp,)),
        ],
        compiler_params=pltpu.CompilerParams(
            collective_id=0, has_side_effects=True, vmem_limit_bytes=40 * 1024 * 1024
        ),
    )(embeddings, labels.reshape(1, row_count), ranks.reshape(1, row_count))
    return out.reshape(row_count)


def solution(mesh):
    placed = (P(("dp", "co"), None), P(("dp", "co")), P(("dp", "co")))
    n_dp, n_co = mesh.shape["dp"], mesh.shape["co"]

    def whole(embeddings, labels, ranks):
        row_count = embeddings.shape[0] // (n_dp * n_co)
        cap = max(2, 2 * row_count // n_dp)
        fits = cap % 8 == 0 and cap <= 128 and n_dp % 4 == 0 and n_co % 2 == 0
        body = functools.partial(local_fused, n_dp, n_co) if fits else local
        return jax.shard_map(
            body, mesh=mesh, in_specs=placed, out_specs=P(("dp", "co")), check_vma=False
        )(embeddings, labels, ranks)

    return whole
```

```python
import functools

import jax
import jax.numpy as jnp
from jax import lax
from jax.experimental import pallas as pl
from jax.experimental.pallas import tpu as pltpu
from jax.sharding import PartitionSpec as P

CL_DEV = 8


EPSILON = 1e-06


def match_best(best, mine_rows, mine_label, mine_rank, other_rows, other_label, other_rank):
    scores = lax.dot_general(
        mine_rows, other_rows, (((1,), (1,)), ((), ())), preferred_element_type=jnp.float32
    )
    linked = (
        (mine_label[:, None] == other_label[None, :])
        & (other_label[None, :] >= 0)
        & (other_rank[None, :] < mine_rank[:, None])
    )
    return jnp.maximum(best, jnp.max(jnp.where(linked, scores, -1.0), axis=1))


def local(embeddings, labels, ranks):
    row_count, width = embeddings.shape
    owner_count = lax.axis_size("dp")
    slot_cap = max(2, 2 * row_count // owner_count)
    slot_total = owner_count * slot_cap
    values = embeddings.astype(jnp.float32)
    unit = (values * lax.rsqrt(jnp.sum(values * values, axis=1, keepdims=True) + EPSILON)).astype(
        jnp.bfloat16
    )
    owner = labels // CL_DEV
    onehot = (owner[:, None] == jnp.arange(owner_count, dtype=jnp.int32)[None, :]).astype(
        jnp.float32
    )
    lower = (jnp.arange(row_count)[:, None] >= jnp.arange(row_count)[None, :]).astype(jnp.float32)
    running = jnp.dot(lower, onehot, preferred_element_type=jnp.float32)
    position = (jnp.sum(running * onehot, axis=1) - 1.0).astype(jnp.int32)
    slot = owner * slot_cap + position
    send_rows = (
        jnp.zeros((slot_total, width), jnp.bfloat16)
        .at[slot]
        .set(unit)
        .reshape(owner_count, slot_cap, width)
    )
    send_label = (
        jnp.full((slot_total,), -1, jnp.int32).at[slot].set(labels).reshape(owner_count, slot_cap)
    )
    send_rank = (
        jnp.zeros((slot_total,), jnp.int32).at[slot].set(ranks).reshape(owner_count, slot_cap)
    )
    start_best = jnp.full((slot_total,), -1.0, jnp.float32)
    group_rows, group_label, group_rank = (
        lax.all_gather(send_rows, "co", axis=1, tiled=True),
        lax.all_gather(send_label, "co", axis=1, tiled=True),
        lax.all_gather(send_rank, "co", axis=1, tiled=True),
    )
    got_rows, got_label, got_rank = (
        lax.all_to_all(group_rows, "dp", split_axis=0, concat_axis=0, tiled=True),
        lax.all_to_all(group_label, "dp", split_axis=0, concat_axis=0, tiled=True),
        lax.all_to_all(group_rank, "dp", split_axis=0, concat_axis=0, tiled=True),
    )
    offset = lax.axis_index("co") * slot_cap
    mine_rows = lax.dynamic_slice_in_dim(got_rows, offset, slot_cap, 1).reshape(slot_total, width)
    mine_label = lax.dynamic_slice_in_dim(got_label, offset, slot_cap, 1).reshape(slot_total)
    mine_rank = lax.dynamic_slice_in_dim(got_rank, offset, slot_cap, 1).reshape(slot_total)
    best = match_best(
        start_best,
        mine_rows,
        mine_label,
        mine_rank,
        got_rows.reshape(-1, width),
        got_label.reshape(-1),
        got_rank.reshape(-1),
    )
    returned = lax.all_to_all(
        best.reshape(owner_count, slot_cap), "dp", split_axis=0, concat_axis=0, tiled=True
    )
    return returned.reshape(slot_total)[slot]


MESH = pl.DeviceIdType.MESH
HIGHEST = lax.Precision.HIGHEST


def iota(shape, dim):
    return lax.broadcasted_iota(jnp.int32, shape, dim)


def owner_place(owner, n_dp, n_co):
    half = n_dp // 2
    return n_dp // 4 + lax.rem(owner, half), (owner // half) * (n_co // 2) + 1


def kernel(
    n_dp, n_co, cap, shift,
    emb_hbm, label_hbm, rank_hbm, out_ref,
    emb_ref, label_ref, rank_ref, fetch_sem,
    send, recv, key_send, key_recv, rows, ret_send, ret_recv,
    send_sem, recv_sem, key_send_sem, key_recv_sem, ret_send_sem, ret_recv_sem,
):
    n_dev = n_dp * n_co
    n_owner = n_dp
    row_count, width = emb_ref.shape
    half = width // 2
    total = n_dev * cap
    my_dp, my_co = lax.axis_index("dp"), lax.axis_index("co")
    me = my_dp * n_co + my_co
    mid = n_dp // 4
    is_owner = (my_dp >= mid) & (my_dp < mid + n_dp // 2) & (lax.rem(my_co, n_co // 2) == 1)
    my_owner = (my_co // (n_co // 2)) * (n_dp // 2) + my_dp - mid

    fetches = [
        pltpu.make_async_copy(a, b, fetch_sem.at[i])
        for i, (a, b) in enumerate(
            ((emb_hbm, emb_ref), (label_hbm, label_ref), (rank_hbm, rank_ref))
        )
    ]
    for fetch in fetches:
        fetch.start()
    barrier = pltpu.get_barrier_semaphore()

    def greet(j, _):
        @pl.when(j != me)
        def _():
            pl.semaphore_signal(
                barrier, inc=1, device_id=(j // n_co, lax.rem(j, n_co)), device_id_type=MESH
            )
        return 0

    @pl.when(is_owner)
    def _():
        lax.fori_loop(0, n_dev, greet, 0)

    @pl.when(jnp.logical_not(is_owner))
    def _():
        def greet_owner(o, _):
            pl.semaphore_signal(
                barrier, inc=1, device_id=owner_place(o, n_dp, n_co), device_id_type=MESH
            )
            return 0

        lax.fori_loop(0, n_owner, greet_owner, 0)

    for fetch in fetches:
        fetch.wait()
    values = emb_ref[...].astype(jnp.float32)
    unit = (values * lax.rsqrt(jnp.sum(values * values, axis=1, keepdims=True) + EPSILON)).astype(
        jnp.bfloat16
    )
    square = (row_count, row_count)
    down, across = iota(square, 0), iota(square, 1)
    label_row = label_ref[...]
    key_row = label_row * (1 << shift) + rank_ref[...]
    owner_row = label_row // CL_DEV
    diagonal = down == across

    def to_column(row):
        return jnp.sum(jnp.where(diagonal, row, 0), axis=1, keepdims=True)

    owner_col, key_col = to_column(owner_row), to_column(key_row)
    same = owner_col == owner_row
    place_row = jnp.sum(jnp.where(same & (down < across), 1, 0), axis=0, keepdims=True)
    place_col = jnp.sum(jnp.where(same & (across < down), 1, 0), axis=1, keepdims=True)

    def to_owner(step):
        owner = lax.rem(me + step, n_owner)
        dp, co = owner_place(owner, n_dp, n_co)
        here = (dp == my_dp) & (co == my_co)
        copies = [
            pltpu.make_async_remote_copy(
                src_ref=a.at[step], dst_ref=b.at[me], send_sem=x.at[step], recv_sem=y.at[me],
                device_id=(dp, co), device_id_type=MESH,
            )
            for a, b, x, y in (
                (key_send, key_recv, key_send_sem, key_recv_sem),
                (send, recv, send_sem, recv_sem),
            )
        ]
        local_copies = [
            pltpu.make_async_copy(a.at[step], b.at[me], y.at[me])
            for a, b, y in ((key_send, key_recv, key_recv_sem), (send, recv, recv_sem))
        ]
        return here, copies, local_copies

    lane = iota((row_count, 128), 1)
    my_sublane = iota((8, 128), 0) == lax.rem(me, 8)
    slot = iota((2 * cap, row_count), 0)
    for step in range(n_owner):
        owner = lax.rem(me + step, n_owner)
        keys = jnp.sum(
            jnp.where((owner_col == owner) & (place_col == lane), key_col + 1, 0),
            axis=0, keepdims=True,
        ) - 1
        key_send[step] = jnp.where(my_sublane, keys, 0).astype(jnp.float32)
        position = jnp.where(owner_row == owner, place_row, -2 * cap)
        low = jnp.where(slot == position, 1.0, 0.0).astype(jnp.bfloat16)
        high = jnp.where(slot == position + cap, 1.0, 0.0).astype(jnp.bfloat16)
        picked = jnp.dot(low, unit[:, :half], preferred_element_type=jnp.float32) + jnp.dot(
            high, unit[:, half:], preferred_element_type=jnp.float32
        )
        send[step] = picked.astype(jnp.bfloat16)

    @pl.when(is_owner)
    def _():
        pl.semaphore_wait(barrier, n_dev - 1)

    @pl.when(jnp.logical_not(is_owner))
    def _():
        pl.semaphore_wait(barrier, n_owner)

    for step in range(n_owner):
        here, copies, local_copies = to_owner(step)

        @pl.when(here)
        def _():
            for copy in local_copies:
                copy.start()

        @pl.when(jnp.logical_not(here))
        def _():
            for copy in copies:
                copy.start()

    @pl.when(is_owner)
    def _():
        every = iota((128, total), 1)
        source = jnp.floor((every.astype(jnp.float32) + 0.5) * (1.0 / cap)).astype(jnp.int32)
        spread = jnp.where(every - source * cap == iota((128, total), 0), 1.0, 0.0)
        every_t = iota((total, 128), 0)
        source_t = jnp.floor((every_t.astype(jnp.float32) + 0.5) * (1.0 / cap)).astype(jnp.int32)
        spread_t = jnp.where(every_t - source_t * cap == iota((total, 128), 1), 1.0, 0.0)
        from_row = source[:n_dev] == iota((n_dev, total), 0)
        from_col = source_t[:, :n_dev] == iota((total, n_dev), 1)

        def wait(kind, sem):
            def one(j, _):
                pltpu.make_async_copy(kind.at[j], kind.at[j], sem.at[j]).wait()
                return 0

            return one

        lax.fori_loop(0, n_dev, wait(key_recv, key_recv_sem), 0)
        table = jnp.sum(key_recv[...].reshape(n_dev // 8, 8, 8, 128), axis=1).reshape(n_dev, 128)
        keys_row = jnp.sum(
            jnp.where(
                from_row,
                jnp.dot(table, spread, precision=HIGHEST, preferred_element_type=jnp.float32),
                0.0,
            ),
            axis=0, keepdims=True,
        )
        keys_col = jnp.sum(
            jnp.where(
                from_col,
                lax.dot_general(
                    spread_t, table, (((1,), (1,)), ((), ())),
                    precision=HIGHEST, preferred_element_type=jnp.float32,
                ),
                0.0,
            ),
            axis=1, keepdims=True,
        )
        keys_row = jnp.round(keys_row)
        keys_col = jnp.round(keys_col)
        first_row = jnp.floor(keys_row * (1.0 / (1 << shift))) * (1 << shift)
        first_row = jnp.maximum(first_row, 0.0)

        for pair in range(n_dev // 2):
            two = []
            for j in (2 * pair, 2 * pair + 1):
                pltpu.make_async_copy(recv.at[j], recv.at[j], recv_sem.at[j]).wait()
                two.append(recv[j].astype(jnp.float32))
            block = pl.ds(pair * 2 * cap, 2 * cap)
            rows[block, :half] = jnp.concatenate([x[:cap] for x in two], axis=0).astype(jnp.bfloat16)
            rows[block, half:] = jnp.concatenate([x[cap:] for x in two], axis=0).astype(jnp.bfloat16)

        best = jnp.full((1, total), -1.0, jnp.float32)
        tall = total // 3 if total % 48 == 0 else total
        for begin in range(0, total, tall):
            scores = lax.dot_general(
                rows[begin : begin + tall, :], rows[...], (((1,), (1,)), ((), ())),
                preferred_element_type=jnp.float32,
            )
            other = keys_col[begin : begin + tall]
            linked = (other < keys_row) & (other >= first_row)
            best = jnp.maximum(
                best, jnp.max(jnp.where(linked, scores, -1.0), axis=0, keepdims=True)
            )
        ret_send[...] = lax.dot_general(
            jnp.where(from_row, best, 0.0), spread, (((1,), (1,)), ((), ())),
            precision=HIGHEST, preferred_element_type=jnp.float32,
        ).reshape(n_dev // 8, 8, 128)

        def back(j):
            return pltpu.make_async_remote_copy(
                src_ref=ret_send.at[j // 8], dst_ref=ret_recv.at[my_owner],
                send_sem=ret_send_sem.at[j], recv_sem=ret_recv_sem.at[my_owner],
                device_id=(j // n_co, lax.rem(j, n_co)), device_id_type=MESH,
            )

        def home(j):
            return pltpu.make_async_copy(
                ret_send.at[j // 8], ret_recv.at[my_owner], ret_recv_sem.at[my_owner]
            )

        def give(j, _):
            @pl.when(j != me)
            def _():
                back(j).start()

            @pl.when(j == me)
            def _():
                home(j).start()
            return 0

        lax.fori_loop(0, n_dev, give, 0)

        def given(j, _):
            @pl.when(j != me)
            def _():
                back(j).wait_send()
            return 0

        lax.fori_loop(0, n_dev, given, 0)

    for step in range(n_owner):
        here, copies, _ = to_owner(step)

        @pl.when(jnp.logical_not(here))
        def _():
            for copy in copies:
                copy.wait_send()

    for o in range(n_owner):
        pltpu.make_async_copy(ret_recv.at[o], ret_recv.at[o], ret_recv_sem.at[o]).wait()
    mine = jnp.sum(jnp.where(my_sublane[None], ret_recv[...], 0.0), axis=1)
    chosen = jnp.where(owner_row == iota((n_owner, row_count), 0), 1.0, 0.0)
    by_place = lax.dot_general(
        mine, chosen, (((0,), (0,)), ((), ())),
        precision=HIGHEST, preferred_element_type=jnp.float32,
    )
    out_ref[...] = jnp.sum(
        jnp.where(iota((128, row_count), 0) == place_row, by_place, 0.0), axis=0, keepdims=True
    )


def local_fused(n_dp, n_co, embeddings, labels, ranks):
    row_count, width = embeddings.shape
    cap = max(2, 2 * row_count // n_dp)
    n_dev = n_dp * n_co
    shift = (row_count * n_dev - 1).bit_length()
    dma = pltpu.SemaphoreType.DMA
    out = pl.pallas_call(
        functools.partial(kernel, n_dp, n_co, cap, shift),
        out_shape=jax.ShapeDtypeStruct((1, row_count), jnp.float32),
        in_specs=[pl.BlockSpec(memory_space=pltpu.HBM)] * 3,
        out_specs=pl.BlockSpec(memory_space=pltpu.VMEM),
        scratch_shapes=[
            pltpu.VMEM((row_count, width), jnp.bfloat16),
            pltpu.VMEM((1, row_count), jnp.int32),
            pltpu.VMEM((1, row_count), jnp.int32),
            dma((3,)),
            pltpu.VMEM((n_dp, 2 * cap, width // 2), jnp.bfloat16),
            pltpu.VMEM((n_dev, 2 * cap, width // 2), jnp.bfloat16),
            pltpu.VMEM((n_dp, 8, 128), jnp.float32),
            pltpu.VMEM((n_dev, 8, 128), jnp.float32),
            pltpu.VMEM((n_dev * cap, width), jnp.bfloat16),
            pltpu.VMEM((n_dev // 8, 8, 128), jnp.float32),
            pltpu.VMEM((n_dp, 8, 128), jnp.float32),
            dma((n_dp,)), dma((n_dev,)), dma((n_dp,)), dma((n_dev,)), dma((n_dev,)), dma((n_dp,)),
        ],
        compiler_params=pltpu.CompilerParams(
            collective_id=0, has_side_effects=True, vmem_limit_bytes=63 * 1024 * 1024
        ),
    )(embeddings, labels.reshape(1, row_count), ranks.reshape(1, row_count))
    return out.reshape(row_count)


def solution(mesh):
    placed = (P(("dp", "co"), None), P(("dp", "co")), P(("dp", "co")))
    n_dp, n_co = mesh.shape["dp"], mesh.shape["co"]

    def whole(embeddings, labels, ranks):
        row_count = embeddings.shape[0] // (n_dp * n_co)
        cap = max(2, 2 * row_count // n_dp)
        fits = cap % 8 == 0 and cap <= 128 and n_dp % 4 == 0 and n_co % 4 == 0
        body = functools.partial(local_fused, n_dp, n_co) if fits else local
        return jax.shard_map(
            body, mesh=mesh, in_specs=placed, out_specs=P(("dp", "co")), check_vma=False
        )(embeddings, labels, ranks)

    return whole
```
